32 devices in a mesh: req: 8 (over z, x), tp: 4 (over y, core).
Axes of the slice: x: 2, y: 2, z: 4, core: 2. Of those that a mesh axis runs over, the one named last changes fastest.
Arguments:
- patches: bfloat16 [8192, 1408], P('req')
- segment_ids: int32 [8192], P('req'), may hold values from 0 to 15, as said below
- grid_sides: int32 [8192], P('req'), may hold values from 8 to 32, as said below
- split_plan: int32 [8, 2], P('req'), may hold values from 0 to 960, as said below
- owner_dev: int32 [2048], P('req'), may hold values from 0 to 7, as said below
- dest_row: int32 [2048], P('req'), may hold values from 0 to 255, as said below
- ln_gain: float32 [1408], replicated, may hold values from 0.25 to 1.75
- ln_bias: float32 [1408], replicated, may hold values from -3 to 3
- w_qkv: bfloat16 [3, 1408, 1408], P(None, 'tp')
- w_out: bfloat16 [1408, 1408], P('tp'), may hold values from -0.625 to 0.625
- w_proj: bfloat16 [5632, 2048], P(None, 'tp'), may hold values from -0.078125 to 0.078125
Outputs:
- vision_tokens: bfloat16 [2048, 2048], P('req', 'tp')
The draws below stay inside these ranges and needn't reach their ends.
Inputs may be any that keep to these rules, and one draw needn't show every extreme that they name: `segment_ids`: within each packed row the ids start at 0, never fall, and one id's patches are contiguous; an image with grid side s has s * s patches (the last image of the whole packing may be cut short) and lies in at most two neighbouring rows. `grid_sides`: all patches of one image share its grid side, a multiple of 8. split_plan[r, 0] is the number of patches of row r's first image that lie in row r - 1, split_plan[r, 1] the number of patches of row r's last image that lie in row r + 1; both are 0 where no image crosses. `owner_dev`: the merged tokens of one row form blocks of 64 consecutive merged tokens; each block goes whole to one owner, a row's blocks go to different owners, and every owner receives 1024 // 4 merged tokens. `dest_row`: every row of every owner's output receives exactly one merged token.
All inputs are finite; a program needn't handle non-finite values.
Results may differ from the reference program's by a relative error of at most 0.019.
Values may be sent and summed in bfloat16 or wider, within the bound.
A program may use at most 128 MiB of HBM per device.

```python
import math
import jax
import jax.numpy as jnp
from jax import lax

D = 1408
HEADS = 16
HD = 88
PROJ = 2048
SIDE_MIN = 8
SIDE_MAX = 32
TOK_DEV = 1024
TOKENS = 8192
MERGED = 2048
HEAD_GROUPS = 4
N_REQ = 8


def packing_layout(key):
    base_key = jax.random.fold_in(key, 4242)
    image_count = TOKENS // (SIDE_MIN * SIDE_MIN) + 1
    multiples = jax.random.randint(jax.random.fold_in(base_key, 1), (image_count,), 1, SIDE_MAX // SIDE_MIN + 1).astype(jnp.int32)
    halves = SIDE_MIN // 2 * multiples
    lead_count = TOK_DEV // (SIDE_MAX * SIDE_MAX)
    small_run = TOK_DEV // (SIDE_MIN * SIDE_MIN) - 1
    image_index = jnp.arange(image_count, dtype=jnp.int32)
    halves = jnp.where(image_index < lead_count - 1, SIDE_MAX // 2, halves)
    halves = jnp.where(image_index == lead_count - 1, SIDE_MIN // 2, halves)
    halves = jnp.where(image_index == lead_count, SIDE_MAX // 2, halves)
    halves = jnp.where((image_index > lead_count) & (image_index <= lead_count + small_run), SIDE_MIN // 2, halves).astype(jnp.int32)
    side_list = 2 * halves
    lengths = side_list * side_list
    end_at = jnp.cumsum(lengths).astype(jnp.int32)
    starts = end_at - lengths
    tok_index = jnp.arange(TOKENS, dtype=jnp.int32)
    image_id = jnp.searchsorted(end_at, tok_index, side='right').astype(jnp.int32)
    by_row = image_id.reshape(N_REQ, TOK_DEV)
    row_first = by_row[:, 0]
    row_last = by_row[:, TOK_DEV - 1]
    segment = (by_row - row_first[:, None]).reshape(TOKENS).astype(jnp.int32)
    token_side = side_list[image_id].astype(jnp.int32)
    row_begin = jnp.arange(N_REQ, dtype=jnp.int32) * TOK_DEV
    before = row_begin - starts[row_first]
    after_rows = jnp.maximum(end_at[row_last] - (row_begin + TOK_DEV), 0)
    after_rows = after_rows.at[N_REQ - 1].set(0)
    return (segment, token_side, jnp.stack([before, after_rows], axis=1).astype(jnp.int32))


def return_layout(key):
    base_key = jax.random.fold_in(key, 5151)
    merged_dev = TOK_DEV // 4
    block_count = N_REQ // 2
    block_size = TOK_DEV // (2 * N_REQ)
    offsets = jax.random.permutation(jax.random.fold_in(base_key, 1), N_REQ)[:block_count].astype(jnp.int32)
    merged_index = jnp.arange(MERGED, dtype=jnp.int32)
    device_id = merged_index // merged_dev
    local_index = merged_index % merged_dev
    block_id = local_index // block_size
    owner_id = (device_id + offsets[block_id]) % N_REQ
    slot_id = block_id * block_size + local_index % block_size
    ranked = jax.random.randint(jax.random.fold_in(base_key, 2), (N_REQ, merged_dev), 0, 1 << 20).astype(jnp.int32) * merged_dev + jnp.arange(merged_dev, dtype=jnp.int32)[None, :]
    shuffled = jnp.argsort(ranked, axis=1).astype(jnp.int32)
    return (owner_id.astype(jnp.int32), shuffled[owner_id, slot_id].astype(jnp.int32))


def draw_segment_ids(key, part):
    return packing_layout(key)[0]


def draw_grid_sides(key, part):
    return packing_layout(key)[1]


def draw_split_plan(key, part):
    return packing_layout(key)[2]


def draw_owner_dev(key, part):
    return return_layout(key)[0]


def draw_dest_row(key, part):
    return return_layout(key)[1]


def draw_patches(key, part):
    base_key, row_key, col_key = jax.random.split(key, 3)
    entries = jax.random.normal(base_key, (TOKENS, D), jnp.float32)
    row_scale = jnp.exp(jax.random.uniform(row_key, (TOKENS, 1), jnp.float32, math.log(0.3), math.log(3.0)))
    col_scale = jnp.exp(jax.random.uniform(col_key, (1, D), jnp.float32, math.log(0.3), math.log(3.0)))
    values = entries * row_scale * col_scale
    return values.astype(jnp.bfloat16)


def draw_w_qkv(key, part):
    entries = jax.random.normal(key, (3, D, D), jnp.float32) * D ** (-0.5)
    return entries.astype(jnp.bfloat16)


def steps_of(own_key, extent, shards, smallest, high):
    def one(dim, shards_of):
        draws = jax.random.uniform(jax.random.fold_in(jax.random.fold_in(own_key, 6), dim), (shards_of,), jnp.float32, smallest / len(shards), high / len(shards))
        return jnp.repeat(jnp.exp(draws), extent[dim] // shards_of).reshape((-1,) + (1,) * (len(extent) - dim - 1))

    level = one(*shards[0])
    for cut in shards[1:]:
        level = level * one(*cut)
    return level


def normal_values(stream_key, shape, width, reach, cuts=(), held_as=jnp.bfloat16):
    values = jax.random.normal(stream_key, shape, jnp.float32) * width
    if len(cuts) > 0:
        values = steps_of(stream_key, shape, cuts, -0.22, 0.18) * values
    return jnp.clip(values, min=-reach, max=reach).astype(held_as)


def setup_inputs(seed: int = 0) -> dict:
    keys = jax.random.split(jax.random.key(seed), 12)
    patches = draw_patches(jax.random.fold_in(keys[11], 71), 0)
    segment_ids = draw_segment_ids(jax.random.fold_in(keys[11], 71), 0)
    grid_sides = draw_grid_sides(jax.random.fold_in(keys[11], 71), 0)
    split_plan = draw_split_plan(jax.random.fold_in(keys[11], 71), 0)
    owner_dev = draw_owner_dev(jax.random.fold_in(keys[11], 71), 0)
    dest_row = draw_dest_row(jax.random.fold_in(keys[11], 71), 0)
    ln_gain = jnp.clip(1.0 + 0.15 * jax.random.normal(keys[6], (D,), jnp.float32), 0.25, 1.75)
    ln_bias = normal_values(keys[7], (D,), 0.5, 3.0, (), jnp.float32)
    w_qkv = draw_w_qkv(jax.random.fold_in(keys[11], 71), 0)
    w_out = normal_values(keys[9], (D, D), HD ** -0.5, 0.625, ((0, 4),))
    w_proj = normal_values(keys[10], (4 * D, PROJ), (4 * D) ** -0.5, 0.078125, ((1, 4),))
    return {"patches": patches, "segment_ids": segment_ids, "grid_sides": grid_sides, "split_plan": split_plan, "owner_dev": owner_dev, "dest_row": dest_row, "ln_gain": ln_gain, "ln_bias": ln_bias, "w_qkv": w_qkv, "w_out": w_out, "w_proj": w_proj}


def layer_norm(inputs, scale_vec, shift_vec):
    widened = inputs.astype(jnp.float32)
    centred = widened - lax.optimization_barrier(jnp.mean(widened, axis=-1, keepdims=True))
    variance = lax.optimization_barrier(jnp.mean(centred * centred, axis=-1, keepdims=True))
    return (centred * lax.rsqrt(variance + 1e-06) * scale_vec + shift_vec).astype(jnp.bfloat16)

def grid_positions(seg_row, side_row, first_offset):
    row_len = seg_row.shape[0]
    tok_index = jnp.arange(row_len, dtype=jnp.int32)
    boundary = jnp.concatenate([jnp.ones((1,), dtype=bool), seg_row[1:] != seg_row[:-1]])
    seg_start = lax.cummax(jnp.where(boundary, tok_index, 0).astype(jnp.int32), axis=0)
    offset = tok_index - seg_start + jnp.where(seg_row == 0, first_offset, 0).astype(jnp.int32)
    half_side = side_row // 2
    window = offset // 4
    corner = offset % 4
    return (2 * (window // half_side) + corner // 2, 2 * (window % half_side) + corner % 2)

def key_labels(seg_row, plan_row):
    row_len = seg_row.shape[0]
    tok_index = jnp.arange(row_len, dtype=jnp.int32)
    before = jnp.where(tok_index >= row_len - plan_row[0], 0, -1).astype(jnp.int32)
    after_keys = jnp.where(tok_index < plan_row[1], seg_row[row_len - 1], -1).astype(jnp.int32)
    return jnp.concatenate([before, seg_row.astype(jnp.int32), after_keys])

def rotate_pairs(channels, angles, axis_pos):
    quarter = channels.shape[axis_pos] // 2
    first_half = lax.slice_in_dim(channels, 0, quarter, axis=axis_pos)
    second_half = lax.slice_in_dim(channels, quarter, 2 * quarter, axis=axis_pos)
    cosine = jnp.cos(angles)
    sine_tab = jnp.sin(angles)
    return jnp.concatenate([first_half * cosine - second_half * sine_tab, second_half * cosine + first_half * sine_tab], axis=axis_pos)

def apply_rope(channels, row_angles, col_angles, axis_pos):
    half_width = channels.shape[axis_pos] // 2
    row_part = rotate_pairs(lax.slice_in_dim(channels, 0, half_width, axis=axis_pos), row_angles, axis_pos)
    col_part = rotate_pairs(lax.slice_in_dim(channels, half_width, 2 * half_width, axis=axis_pos), col_angles, axis_pos)
    return jnp.concatenate([row_part, col_part], axis=axis_pos)

def reference(patches, segment_ids, grid_sides, split_plan, owner_dev, dest_row, ln_gain, ln_bias, w_qkv, w_out, w_proj):
    row_patches = patches.reshape(N_REQ, TOK_DEV, D)
    row_segments = segment_ids.reshape(N_REQ, TOK_DEV)
    row_sides = grid_sides.reshape(N_REQ, TOK_DEV)
    quarter = HD // 4
    frequency = 10000.0 ** (-jnp.arange(quarter, dtype=jnp.float32) / quarter)
    w_flat = w_qkv.reshape(3 * D, D)

    def project_row(packed):
        patch_row, seg_row, side_row, plan_row = packed
        normed = layer_norm(patch_row, ln_gain, ln_bias)
        mixed_qkv = jnp.dot(normed, w_flat.T, preferred_element_type=jnp.float32).reshape(TOK_DEV, 3, HEADS, HD)
        grid_row, grid_col = grid_positions(seg_row, side_row, plan_row[0])
        row_angles = grid_row.astype(jnp.float32)[:, None, None] * frequency
        col_angles = grid_col.astype(jnp.float32)[:, None, None] * frequency
        queries = apply_rope(mixed_qkv[:, 0], row_angles, col_angles, 2).astype(jnp.bfloat16)
        key_rot = apply_rope(mixed_qkv[:, 1], row_angles, col_angles, 2).astype(jnp.bfloat16)
        return (queries, key_rot, mixed_qkv[:, 2].astype(jnp.bfloat16))
    queries, all_keys, all_values = lax.map(project_row, (row_patches, row_segments, row_sides, split_plan))
    pad_width = ((1, 1), (0, 0), (0, 0), (0, 0))
    keys_pad = jnp.pad(all_keys, pad_width)
    values_pad = jnp.pad(all_values, pad_width)
    group_width = D // HEAD_GROUPS
    w_groups = w_out.reshape(HEAD_GROUPS, group_width, D).astype(jnp.float32)

    def attend_row(packed):
        row_index, patch_row, query_row, seg_row, plan_row = packed
        near_keys = lax.dynamic_slice_in_dim(keys_pad, row_index, 3, 0).reshape(3 * TOK_DEV, HEADS, HD)
        near_values = lax.dynamic_slice_in_dim(values_pad, row_index, 3, 0).reshape(3 * TOK_DEV, HEADS, HD)
        labels = key_labels(seg_row, plan_row)
        allowed = seg_row[:, None] == labels[None, :]
        scores = jnp.einsum('qhc,khc->hqk', query_row.astype(jnp.float32), near_keys.astype(jnp.float32)) * HD ** (-0.5)
        scores = jnp.where(allowed[None], scores, -1e+30)
        largest = lax.optimization_barrier(jnp.max(scores, axis=-1, keepdims=True))
        weights = jnp.exp(scores - largest)
        attn_probs = (weights / lax.optimization_barrier(jnp.sum(weights, axis=-1, keepdims=True))).astype(jnp.bfloat16)
        heads_out = jnp.einsum('hqk,khc->qhc', attn_probs.astype(jnp.float32), near_values.astype(jnp.float32)).astype(jnp.bfloat16)
        grouped = heads_out.reshape(TOK_DEV, HEAD_GROUPS, group_width).astype(jnp.float32)
        partial_value = jnp.einsum('qgc,gcd->gqd', grouped, w_groups).astype(jnp.bfloat16)
        attn_sum = lax.optimization_barrier(jnp.sum(partial_value.astype(jnp.float32), axis=0))
        return (patch_row.astype(jnp.float32) + attn_sum).astype(jnp.bfloat16)
    mixed_rows = lax.map(attend_row, (jnp.arange(N_REQ, dtype=jnp.int32), row_patches, queries, row_segments, split_plan))
    merged = mixed_rows.reshape(MERGED, 4 * D)
    projected = jnp.dot(merged, w_proj, preferred_element_type=jnp.float32).astype(jnp.bfloat16)
    target = owner_dev * (TOK_DEV // 4) + dest_row
    return jnp.zeros((MERGED, PROJ), jnp.bfloat16).at[target].set(projected)
```

```python
import jax
import jax.numpy as jnp
from jax import lax
from jax.experimental import pallas as pl
from jax.experimental.pallas import tpu as pltpu
from jax.sharding import PartitionSpec as P

HD = 88


def layer_norm(inputs, scale_vec, shift_vec):
    widened = inputs.astype(jnp.float32)
    centred = widened - jnp.mean(widened, axis=-1, keepdims=True)
    variance = jnp.mean(centred * centred, axis=-1, keepdims=True)
    return (centred * lax.rsqrt(variance + 1e-06) * scale_vec + shift_vec).astype(jnp.bfloat16)


def grid_positions(seg_row, side_row, first_offset):
    row_len = seg_row.shape[0]
    tok_index = jnp.arange(row_len, dtype=jnp.int32)
    boundary = jnp.concatenate([jnp.ones((1,), dtype=bool), seg_row[1:] != seg_row[:-1]])
    seg_start = lax.cummax(jnp.where(boundary, tok_index, 0), axis=0)
    offset = tok_index - seg_start + jnp.where(seg_row == 0, first_offset, 0)
    half_side = side_row // 2
    window = offset // 4
    corner = offset % 4
    return (2 * (window // half_side) + corner // 2, 2 * (window % half_side) + corner % 2)


def rotate_pairs(channels, angles, axis_pos):
    quarter = channels.shape[axis_pos] // 2
    first_half = lax.slice_in_dim(channels, 0, quarter, axis=axis_pos)
    second_half = lax.slice_in_dim(channels, quarter, 2 * quarter, axis=axis_pos)
    cosine = jnp.cos(angles)
    sine_tab = jnp.sin(angles)
    return jnp.concatenate(
        [
            first_half * cosine - second_half * sine_tab,
            second_half * cosine + first_half * sine_tab,
        ],
        axis=axis_pos,
    )


def apply_rope(channels, row_angles, col_angles, axis_pos):
    half_width = channels.shape[axis_pos] // 2
    row_part = rotate_pairs(
        lax.slice_in_dim(channels, 0, half_width, axis=axis_pos), row_angles, axis_pos
    )
    col_part = rotate_pairs(
        lax.slice_in_dim(channels, half_width, 2 * half_width, axis=axis_pos), col_angles, axis_pos
    )
    return jnp.concatenate([row_part, col_part], axis=axis_pos)


def attend_tile(q_tile, k_ref, v_ref, kt, tile, allowed, state):
    largest, total, acc = state
    keys = k_ref[0, :, pl.ds(kt * tile, tile)]
    vals = v_ref[0, :, pl.ds(kt * tile, tile)]
    scores = lax.dot_general(
        keys, q_tile, (((0,), (0,)), ((), ())), preferred_element_type=jnp.float32
    )
    scores = jnp.where(allowed, scores, -1e30)
    larger = jnp.maximum(largest, jnp.max(scores, axis=0, keepdims=True))
    weights = jnp.exp2(scores - larger)
    decay = jnp.exp2(largest - larger)
    total = total * decay + jnp.sum(weights, axis=0, keepdims=True)
    acc = acc * decay + jnp.dot(
        vals, weights.astype(jnp.bfloat16), preferred_element_type=jnp.float32
    )
    return larger, total, acc


def own_kernel(tile, seg_s, q_ref, k_ref, v_ref, segq_ref, segk_ref, acc_ref, stat_ref):
    qt = pl.program_id(1)
    tiles = k_ref.shape[2] // tile
    q_tile = q_ref[0]
    q_lo, q_hi = (seg_s[qt * tile], seg_s[qt * tile + tile - 1])
    seg_q = segq_ref[...]
    stat_ref[0, 0:1, :] = jnp.full((1, tile), -1e30, jnp.float32)
    stat_ref[0, 1:2, :] = jnp.zeros((1, tile), jnp.float32)
    acc_ref[...] = jnp.zeros_like(acc_ref)
    for kt in range(tiles):
        k_lo, k_hi = (seg_s[kt * tile], seg_s[kt * tile + tile - 1])

        @pl.when((k_lo <= q_hi) & (q_lo <= k_hi))
        def _(kt=kt):
            allowed = segk_ref[kt * tile : (kt + 1) * tile, :] == seg_q
            state = (stat_ref[0, 0:1, :], stat_ref[0, 1:2, :], acc_ref[0])
            largest, total, acc = attend_tile(q_tile, k_ref, v_ref, kt, tile, allowed, state)
            stat_ref[0, 0:1, :] = largest
            stat_ref[0, 1:2, :] = total
            acc_ref[0] = acc


def near_kernel(
    tile, seg_s, plan_s, q_ref, kb_ref, vb_ref, ka_ref, va_ref, segq_ref, acc0_ref, stat0_ref,
    out_ref, stat_ref, acc_ref,
):
    qt = pl.program_id(1)
    length = kb_ref.shape[2]
    tiles = length // tile
    q_tile = q_ref[0]
    q_lo, q_hi, last = (seg_s[qt * tile], seg_s[qt * tile + tile - 1], seg_s[length - 1])
    from_before, from_after = (plan_s[0, 0], plan_s[0, 1])
    seg_q = segq_ref[...]
    stat_ref[...] = stat0_ref[0]
    acc_ref[...] = acc0_ref[0]

    def step(k_ref, v_ref, kt, allowed):
        state = (stat_ref[0:1, :], stat_ref[1:2, :], acc_ref[...])
        largest, total, acc = attend_tile(q_tile, k_ref, v_ref, kt, tile, allowed, state)
        stat_ref[0:1, :] = largest
        stat_ref[1:2, :] = total
        acc_ref[...] = acc

    for kt in range(tiles):
        rows = lax.broadcasted_iota(jnp.int32, (tile, tile), 0) + kt * tile

        @pl.when((q_lo == 0) & ((kt + 1) * tile > length - from_before))
        def _(kt=kt, rows=rows):
            step(kb_ref, vb_ref, kt, (rows >= length - from_before) & (seg_q == 0))

        @pl.when((q_hi == last) & (kt * tile < from_after))
        def _(kt=kt, rows=rows):
            step(ka_ref, va_ref, kt, (rows < from_after) & (seg_q == last))

    out_ref[0] = (acc_ref[...] / stat_ref[1:2, :]).astype(out_ref.dtype)


def attend_own(queries, keys, values, segment_ids, tile):
    heads, width, length = queries.shape
    whole = pl.BlockSpec((1, width, length), lambda h, t, *_: (h, 0, 0))
    tiled = pl.BlockSpec((1, width, tile), lambda h, t, *_: (h, 0, t))
    return pl.pallas_call(
        lambda *refs: own_kernel(tile, *refs),
        out_shape=(
            jax.ShapeDtypeStruct((heads, width, length), jnp.float32),
            jax.ShapeDtypeStruct((heads, 8, length), jnp.float32),
        ),
        grid_spec=pltpu.PrefetchScalarGridSpec(
            num_scalar_prefetch=1,
            grid=(heads, length // tile),
            in_specs=[
                tiled,
                whole,
                whole,
                pl.BlockSpec((1, tile), lambda h, t, *_: (0, t)),
                pl.BlockSpec((length, 1), lambda h, t, *_: (0, 0)),
            ],
            out_specs=(tiled, pl.BlockSpec((1, 8, tile), lambda h, t, *_: (h, 0, t))),
        ),
        compiler_params=pltpu.CompilerParams(vmem_limit_bytes=32 * 2**20),
        cost_estimate=pl.CostEstimate(
            flops=4 * heads * length * length * width,
            bytes_accessed=4 * heads * length * width * 2,
            transcendentals=heads * length * length,
        ),
        name="own_attention",
    )(segment_ids, queries, keys, values, segment_ids[None, :], segment_ids[:, None])


def attend_near(queries, before, after, segment_ids, split_plan, acc, stat, tile):
    heads, width, length = queries.shape
    whole = pl.BlockSpec((1, width, length), lambda h, t, *_: (h, 0, 0))
    tiled = pl.BlockSpec((1, width, tile), lambda h, t, *_: (h, 0, t))
    return pl.pallas_call(
        lambda *refs: near_kernel(tile, *refs),
        out_shape=jax.ShapeDtypeStruct((heads, width, length), jnp.bfloat16),
        grid_spec=pltpu.PrefetchScalarGridSpec(
            num_scalar_prefetch=2,
            grid=(heads, length // tile),
            in_specs=[
                tiled,
                whole,
                whole,
                whole,
                whole,
                pl.BlockSpec((1, tile), lambda h, t, *_: (0, t)),
                tiled,
                pl.BlockSpec((1, 8, tile), lambda h, t, *_: (h, 0, t)),
            ],
            out_specs=tiled,
            scratch_shapes=[
                pltpu.VMEM((8, tile), jnp.float32),
                pltpu.VMEM((width, tile), jnp.float32),
            ],
        ),
        compiler_params=pltpu.CompilerParams(vmem_limit_bytes=32 * 2**20),
        cost_estimate=pl.CostEstimate(
            flops=4 * heads * length * length * width,
            bytes_accessed=6 * heads * length * width * 2,
            transcendentals=heads * length * length,
        ),
        name="near_attention",
    )(
        segment_ids, split_plan, queries, before[0], before[1], after[0], after[1],
        segment_ids[None, :], acc, stat,
    )


def mix_kernel(ho_ref, wout_ref, patch_ref, wproj_ref, out_ref, mixed_ref):
    length, width = patch_ref.shape
    block = 256

    def mix(i, carry):
        rows = pl.ds(pl.multiple_of(i * block, block), block)
        total = lax.dot_general(
            ho_ref[:, rows], wout_ref[...], (((0,), (0,)), ((), ())),
            preferred_element_type=jnp.float32,
        )
        total = total + patch_ref[rows, :].astype(jnp.float32)
        for g in range(width // 128):
            mixed_ref[g, rows, :] = total[:, g * 128 : (g + 1) * 128]
        return carry

    lax.fori_loop(0, length // block, mix, 0)
    total = jnp.zeros(out_ref.shape, jnp.float32)
    for corner in range(4):
        part = jnp.concatenate(
            [
                mixed_ref[g, pl.ds(corner, length // 4, stride=4), :].astype(jnp.bfloat16)
                for g in range(width // 128)
            ],
            axis=1,
        )
        total += jnp.dot(
            part,
            wproj_ref[corner * width : (corner + 1) * width, :],
            preferred_element_type=jnp.float32,
        )
    out_ref[...] = total.astype(out_ref.dtype)


def mix_and_project(heads_out, w_out, patches, w_proj):
    length, width = patches.shape
    vmem = pl.BlockSpec(memory_space=pltpu.VMEM)
    return pl.pallas_call(
        mix_kernel,
        out_shape=jax.ShapeDtypeStruct((length // 4, w_proj.shape[1]), jnp.bfloat16),
        in_specs=[vmem] * 4,
        out_specs=vmem,
        scratch_shapes=[pltpu.VMEM((width // 128, length, 128), jnp.float32)],
        compiler_params=pltpu.CompilerParams(vmem_limit_bytes=48 * 2**20),
        name="mix_and_project",
    )(heads_out, w_out, patches, w_proj)


def on_device(
    patches,
    segment_ids,
    grid_sides,
    split_plan,
    owner_dev,
    dest_row,
    ln_gain,
    ln_bias,
    w_qkv,
    w_out,
    w_proj,
):
    tok_count = patches.shape[0]
    local_heads = w_qkv.shape[1] // HD
    tile = min(256, tok_count)
    w_out_all = lax.all_gather(w_out, "tp", axis=0, tiled=True)
    normed = layer_norm(patches, ln_gain, ln_bias)
    grid_row, grid_col = grid_positions(segment_ids, grid_sides, split_plan[0, 0])
    quarter = HD // 4
    frequency = 10000.0 ** (-jnp.arange(quarter, dtype=jnp.float32) / quarter)
    row_angles = frequency[:, None] * grid_row.astype(jnp.float32)[None, :]
    col_angles = frequency[:, None] * grid_col.astype(jnp.float32)[None, :]
    mixed_kv = jnp.einsum("td,kcd->kct", normed, w_qkv[1:], preferred_element_type=jnp.float32)
    shaped = mixed_kv.reshape(2, local_heads, HD, tok_count)
    keys = apply_rope(shaped[0], row_angles, col_angles, 1).astype(jnp.bfloat16)
    values = shaped[1].astype(jnp.bfloat16)
    count = lax.axis_size("req")
    up = [(i, i + 1) for i in range(count - 1)]
    down = [(j, i) for i, j in up]
    before = [lax.ppermute(part, "req", up) for part in (keys, values)]
    after = [lax.ppermute(part, "req", down) for part in (keys, values)]
    mixed_q = jnp.einsum("td,cd->ct", normed, w_qkv[0], preferred_element_type=jnp.float32)
    mixed_q = mixed_q.reshape(local_heads, HD, tok_count)
    scale = HD ** (-0.5) * 1.4426950408889634
    queries = (apply_rope(mixed_q, row_angles, col_angles, 1) * scale).astype(jnp.bfloat16)
    acc, stat = attend_own(queries, keys, values, segment_ids, tile)
    heads_out = attend_near(queries, before, after, segment_ids, split_plan, acc, stat, tile)
    heads_all = lax.all_gather(
        heads_out.reshape(local_heads * HD, tok_count), "tp", axis=0, tiled=True
    )
    projected = mix_and_project(heads_all, w_out_all, patches, w_proj)
    per_owner = owner_dev.shape[0]
    peer_count = lax.axis_size("req")
    owner_slots = 2 * per_owner // peer_count
    matches = (owner_dev[:, None] == jnp.arange(peer_count, dtype=jnp.int32)[None, :]).astype(
        jnp.int32
    )
    arrival = jnp.sum(jnp.cumsum(matches, axis=0) * matches, axis=1) - 1
    send_slot = owner_dev * owner_slots + arrival
    slots = jnp.arange(peer_count * owner_slots, dtype=jnp.int32)
    hit = slots[:, None] == send_slot[None, :]
    send_dest = jnp.sum(jnp.where(hit, dest_row[None, :] + 1, 0), axis=1) - 1
    got_dest = lax.all_to_all(send_dest, "req", split_axis=0, concat_axis=0, tiled=True)
    place = (jnp.arange(per_owner, dtype=jnp.int32)[:, None] == got_dest[None, :]).astype(
        jnp.bfloat16
    )
    send_rows = jnp.dot(
        hit.astype(jnp.bfloat16), projected, preferred_element_type=jnp.float32
    ).astype(jnp.bfloat16)
    got_rows = lax.all_to_all(send_rows, "req", split_axis=0, concat_axis=0, tiled=True)
    return jnp.dot(place, got_rows, preferred_element_type=jnp.float32).astype(jnp.bfloat16)


def solution(mesh):
    placed = (
        P("req", None),
        P("req"),
        P("req"),
        P("req", None),
        P("req"),
        P("req"),
        P(),
        P(),
        P(None, "tp", None),
        P("tp", None),
        P(None, "tp"),
    )
    return jax.shard_map(
        on_device, mesh=mesh, in_specs=placed, out_specs=P("req", "tp"), check_vma=False
    )
```

```python
import jax
import jax.numpy as jnp
from jax import lax
from jax.experimental import pallas as pl
from jax.experimental.pallas import tpu as pltpu
from jax.sharding import PartitionSpec as P

HD = 88


def layer_norm(inputs, scale_vec, shift_vec):
    widened = inputs.astype(jnp.float32)
    centred = widened - jnp.mean(widened, axis=-1, keepdims=True)
    variance = jnp.mean(centred * centred, axis=-1, keepdims=True)
    return (centred * lax.rsqrt(variance + 1e-06) * scale_vec + shift_vec).astype(jnp.bfloat16)


def grid_positions(seg_row, side_row, first_offset):
    row_len = seg_row.shape[0]
    tok_index = jnp.arange(row_len, dtype=jnp.int32)
    boundary = jnp.concatenate([jnp.ones((1,), dtype=bool), seg_row[1:] != seg_row[:-1]])
    seg_start = lax.cummax(jnp.where(boundary, tok_index, 0), axis=0)
    offset = tok_index - seg_start + jnp.where(seg_row == 0, first_offset, 0)
    half_side = side_row // 2
    window = offset // 4
    corner = offset % 4
    return (2 * (window // half_side) + corner // 2, 2 * (window % half_side) + corner % 2)


def rotate_pairs(channels, angles, axis_pos):
    quarter = channels.shape[axis_pos] // 2
    first_half = lax.slice_in_dim(channels, 0, quarter, axis=axis_pos)
    second_half = lax.slice_in_dim(channels, quarter, 2 * quarter, axis=axis_pos)
    cosine = jnp.cos(angles)
    sine_tab = jnp.sin(angles)
    return jnp.concatenate(
        [
            first_half * cosine - second_half * sine_tab,
            second_half * cosine + first_half * sine_tab,
        ],
        axis=axis_pos,
    )


def apply_rope(channels, row_angles, col_angles, axis_pos):
    half_width = channels.shape[axis_pos] // 2
    row_part = rotate_pairs(
        lax.slice_in_dim(channels, 0, half_width, axis=axis_pos), row_angles, axis_pos
    )
    col_part = rotate_pairs(
        lax.slice_in_dim(channels, half_width, 2 * half_width, axis=axis_pos), col_angles, axis_pos
    )
    return jnp.concatenate([row_part, col_part], axis=axis_pos)


def attend_tile(q_tile, k_ref, v_ref, head, kt, tile, allowed, state):
    largest, total, acc = state
    keys = k_ref[head, :, pl.ds(kt * tile, tile)]
    vals = v_ref[head, :, pl.ds(kt * tile, tile)]
    scores = lax.dot_general(
        keys, q_tile, (((0,), (0,)), ((), ())), preferred_element_type=jnp.float32
    )
    scores = jnp.where(allowed, scores, -1e30)
    larger = jnp.maximum(largest, jnp.max(scores, axis=0, keepdims=True))
    weights = jnp.exp2(scores - larger)
    decay = jnp.exp2(largest - larger)
    total = total * decay + jnp.sum(weights, axis=0, keepdims=True)
    acc = acc * decay + jnp.dot(
        vals, weights.astype(jnp.bfloat16), preferred_element_type=jnp.float32
    )
    return larger, total, acc


def own_kernel(tile, seg_s, q_ref, k_ref, v_ref, segq_ref, segk_ref, acc_ref, stat_ref):
    qt = pl.program_id(0)
    heads = q_ref.shape[0]
    tiles = k_ref.shape[2] // tile
    q_lo, q_hi = (seg_s[qt * tile], seg_s[qt * tile + tile - 1])
    seg_q = segq_ref[...]
    stat_ref[:, 0:1, :] = jnp.full((heads, 1, tile), -1e30, jnp.float32)
    stat_ref[:, 1:8, :] = jnp.zeros((heads, 7, tile), jnp.float32)
    acc_ref[...] = jnp.zeros_like(acc_ref)
    for kt in range(tiles):
        k_lo, k_hi = (seg_s[kt * tile], seg_s[kt * tile + tile - 1])

        @pl.when((k_lo <= q_hi) & (q_lo <= k_hi))
        def _(kt=kt):
            allowed = segk_ref[kt * tile : (kt + 1) * tile, :] == seg_q
            states = [
                attend_tile(
                    q_ref[h], k_ref, v_ref, h, kt, tile, allowed,
                    (stat_ref[h, 0:1, :], stat_ref[h, 1:2, :], acc_ref[h]),
                )
                for h in range(heads)
            ]
            for h, (largest, total, acc) in enumerate(states):
                stat_ref[h, 0:1, :] = largest
                stat_ref[h, 1:2, :] = total
                acc_ref[h] = acc


def near_kernel(
    tile, seg_s, plan_s, q_ref, before_ref, after_ref, segq_ref, acc0_ref, stat0_ref,
    out_ref, stat_ref, acc_ref,
):
    qt = pl.program_id(0)
    heads = q_ref.shape[0]
    length = before_ref.shape[3]
    tiles = length // tile
    q_lo, q_hi, last = (seg_s[qt * tile], seg_s[qt * tile + tile - 1], seg_s[length - 1])
    from_before, from_after = (plan_s[0, 0], plan_s[0, 1])
    seg_q = segq_ref[...]
    stat_ref[...] = stat0_ref[...]
    acc_ref[...] = acc0_ref[...]

    def step(kv_ref, kt, allowed):
        states = [
            attend_tile(
                q_ref[h], kv_ref.at[0], kv_ref.at[1], h, kt, tile, allowed,
                (stat_ref[h, 0:1, :], stat_ref[h, 1:2, :], acc_ref[h]),
            )
            for h in range(heads)
        ]
        for h, (largest, total, acc) in enumerate(states):
            stat_ref[h, 0:1, :] = largest
            stat_ref[h, 1:2, :] = total
            acc_ref[h] = acc

    for kt in range(tiles):

        @pl.when((q_lo == 0) & ((kt + 1) * tile > length - from_before))
        def _(kt=kt):
            rows = lax.broadcasted_iota(jnp.int32, (tile, tile), 0) + kt * tile
            step(before_ref, kt, (rows >= length - from_before) & (seg_q == 0))

        @pl.when((q_hi == last) & (kt * tile < from_after))
        def _(kt=kt):
            rows = lax.broadcasted_iota(jnp.int32, (tile, tile), 0) + kt * tile
            step(after_ref, kt, (rows < from_after) & (seg_q == last))

    for h in range(heads):
        out_ref[h] = (acc_ref[h] / stat_ref[h, 1:2, :]).astype(out_ref.dtype)


def attend_own(queries, keys, values, segment_ids, tile):
    heads, width, length = queries.shape
    whole = pl.BlockSpec((heads, width, length), lambda t, *_: (0, 0, 0))
    tiled = pl.BlockSpec((heads, width, tile), lambda t, *_: (0, 0, t))
    return pl.pallas_call(
        lambda *refs: own_kernel(tile, *refs),
        out_shape=(
            jax.ShapeDtypeStruct((heads, width, length), jnp.float32),
            jax.ShapeDtypeStruct((heads, 8, length), jnp.float32),
        ),
        grid_spec=pltpu.PrefetchScalarGridSpec(
            num_scalar_prefetch=1,
            grid=(length // tile,),
            in_specs=[
                tiled,
                whole,
                whole,
                pl.BlockSpec((1, tile), lambda t, *_: (0, t)),
                pl.BlockSpec((length, 1), lambda t, *_: (0, 0)),
            ],
            out_specs=(tiled, pl.BlockSpec((heads, 8, tile), lambda t, *_: (0, 0, t))),
        ),
        compiler_params=pltpu.CompilerParams(vmem_limit_bytes=32 * 2**20),
        cost_estimate=pl.CostEstimate(
            flops=4 * heads * length * length * width,
            bytes_accessed=4 * heads * length * width * 2,
            transcendentals=heads * length * length,
        ),
        name="own_attention",
    )(segment_ids, queries, keys, values, segment_ids[None, :], segment_ids[:, None])


def attend_near(queries, before, after, segment_ids, split_plan, acc, stat, tile, part):
    _, heads, width, length = before.shape
    whole = pl.BlockSpec((2, heads, width, length), lambda t, *_: (0, 0, 0, 0))
    tiled = pl.BlockSpec((heads, width, tile), lambda t, *_: (part, 0, t))
    return pl.pallas_call(
        lambda *refs: near_kernel(tile, *refs),
        out_shape=jax.ShapeDtypeStruct((heads, width, length), jnp.bfloat16),
        grid_spec=pltpu.PrefetchScalarGridSpec(
            num_scalar_prefetch=2,
            grid=(length // tile,),
            in_specs=[
                tiled,
                whole,
                whole,
                pl.BlockSpec((1, tile), lambda t, *_: (0, t)),
                tiled,
                pl.BlockSpec((heads, 8, tile), lambda t, *_: (part, 0, t)),
            ],
            out_specs=pl.BlockSpec((heads, width, tile), lambda t, *_: (0, 0, t)),
            scratch_shapes=[
                pltpu.VMEM((heads, 8, tile), jnp.float32),
                pltpu.VMEM((heads, width, tile), jnp.float32),
            ],
        ),
        compiler_params=pltpu.CompilerParams(vmem_limit_bytes=32 * 2**20),
        cost_estimate=pl.CostEstimate(
            flops=4 * heads * length * length * width,
            bytes_accessed=6 * heads * length * width * 2,
            transcendentals=heads * length * length,
        ),
        name="near_attention",
    )(
        segment_ids, split_plan, queries, before, after,
        segment_ids[None, :], acc, stat,
    )


def mix_kernel(ho_a_ref, ho_b_ref, wa_ref, wb_ref, patch_ref, wproj_ref, out_ref, mixed_ref):
    length, width = patch_ref.shape
    block = 256

    def mix(i, carry):
        rows = pl.ds(pl.multiple_of(i * block, block), block)
        total = patch_ref[rows, :].astype(jnp.float32)
        for ho_ref, w_ref in ((ho_a_ref, wa_ref), (ho_b_ref, wb_ref)):
            total = total + lax.dot_general(
                ho_ref[:, rows], w_ref[...], (((0,), (0,)), ((), ())),
                preferred_element_type=jnp.float32,
            )
        for g in range(width // 128):
            mixed_ref[g, rows, :] = total[:, g * 128 : (g + 1) * 128]
        return carry

    lax.fori_loop(0, length // block, mix, 0)
    total = jnp.zeros(out_ref.shape, jnp.float32)
    for corner in range(4):
        part = jnp.concatenate(
            [
                mixed_ref[g, pl.ds(corner, length // 4, stride=4), :].astype(jnp.bfloat16)
                for g in range(width // 128)
            ],
            axis=1,
        )
        total += jnp.dot(
            part,
            wproj_ref[corner * width : (corner + 1) * width, :],
            preferred_element_type=jnp.float32,
        )
    out_ref[...] = total.astype(out_ref.dtype)


def mix_and_project(heads_out, w_out, patches, w_proj):
    length, width = patches.shape
    vmem = pl.BlockSpec(memory_space=pltpu.VMEM)
    return pl.pallas_call(
        mix_kernel,
        out_shape=jax.ShapeDtypeStruct((length // 4, w_proj.shape[1]), jnp.bfloat16),
        in_specs=[vmem] * 6,
        out_specs=vmem,
        scratch_shapes=[pltpu.VMEM((width // 128, length, 128), jnp.float32)],
        compiler_params=pltpu.CompilerParams(vmem_limit_bytes=48 * 2**20),
        name="mix_and_project",
    )(*heads_out, *w_out, patches, w_proj)


def on_device(
    patches,
    segment_ids,
    grid_sides,
    split_plan,
    owner_dev,
    dest_row,
    ln_gain,
    ln_bias,
    w_qkv,
    w_out,
    w_proj,
):
    tok_count = patches.shape[0]
    local_heads = w_qkv.shape[1] // HD
    tile = min(256, tok_count)
    split = w_out.shape[0] // 2
    w_out_all = [
        lax.all_gather(part, "tp", axis=0, tiled=True) for part in (w_out[:split], w_out[split:])
    ]
    normed = layer_norm(patches, ln_gain, ln_bias)
    grid_row, grid_col = grid_positions(segment_ids, grid_sides, split_plan[0, 0])
    quarter = HD // 4
    frequency = 10000.0 ** (-jnp.arange(quarter, dtype=jnp.float32) / quarter)
    row_angles = frequency[:, None] * grid_row.astype(jnp.float32)[None, :]
    col_angles = frequency[:, None] * grid_col.astype(jnp.float32)[None, :]
    mixed_kv = jnp.einsum("td,kcd->kct", normed, w_qkv[1:], preferred_element_type=jnp.float32)
    shaped = mixed_kv.reshape(2, local_heads, HD, tok_count)
    keys = apply_rope(shaped[0], row_angles, col_angles, 1).astype(jnp.bfloat16)
    values = shaped[1].astype(jnp.bfloat16)
    count = lax.axis_size("req")
    up = [(i, i + 1) for i in range(count - 1)]
    down = [(j, i) for i, j in up]
    half = local_heads // 2
    near = []
    for first in (0, half):
        part = jnp.stack([keys[first : first + half], values[first : first + half]])
        near.append((lax.ppermute(part, "req", up), lax.ppermute(part, "req", down)))
    mixed_q = jnp.einsum("td,cd->ct", normed, w_qkv[0], preferred_element_type=jnp.float32)
    mixed_q = mixed_q.reshape(local_heads, HD, tok_count)
    scale = HD ** (-0.5) * 1.4426950408889634
    queries = (apply_rope(mixed_q, row_angles, col_angles, 1) * scale).astype(jnp.bfloat16)
    acc, stat = attend_own(queries, keys, values, segment_ids, tile)
    per_owner = owner_dev.shape[0]
    peer_count = lax.axis_size("req")
    owner_slots = 2 * per_owner // peer_count
    matches = (owner_dev[:, None] == jnp.arange(peer_count, dtype=jnp.int32)[None, :]).astype(
        jnp.int32
    )
    arrival = jnp.sum(jnp.cumsum(matches, axis=0) * matches, axis=1) - 1
    send_slot = owner_dev * owner_slots + arrival
    slots = jnp.arange(peer_count * owner_slots, dtype=jnp.int32)
    hit = slots[:, None] == send_slot[None, :]
    send_dest = jnp.sum(jnp.where(hit, dest_row[None, :] + 1, 0), axis=1) - 1
    all_dest = lax.all_gather(send_dest, "req", axis=0, tiled=True)
    all_dest = all_dest.reshape(peer_count, peer_count, owner_slots)
    got_dest = lax.dynamic_index_in_dim(
        all_dest, lax.axis_index("req"), axis=1, keepdims=False
    ).reshape(-1)
    acc, stat, w_out_all, got_dest, near = lax.optimization_barrier(
        (acc, stat, w_out_all, got_dest, near)
    )
    heads_all = []
    for part, (before, after) in enumerate(near):
        heads_out = attend_near(
            queries, before, after, segment_ids, split_plan, acc, stat, tile, part
        )
        heads_all.append(
            lax.all_gather(heads_out.reshape(half * HD, tok_count), "tp", axis=0, tiled=True)
        )
    projected = mix_and_project(heads_all, w_out_all, patches, w_proj)
    place = (jnp.arange(per_owner, dtype=jnp.int32)[:, None] == got_dest[None, :]).astype(
        jnp.bfloat16
    )
    send_rows = jnp.dot(
        hit.astype(jnp.bfloat16), projected, preferred_element_type=jnp.float32
    ).astype(jnp.bfloat16)
    got_rows = lax.all_to_all(send_rows, "req", split_axis=0, concat_axis=0, tiled=True)
    return jnp.dot(place, got_rows, preferred_element_type=jnp.float32).astype(jnp.bfloat16)


def solution(mesh):
    placed = (
        P("req", None),
        P("req"),
        P("req"),
        P("req", None),
        P("req"),
        P("req"),
        P(),
        P(),
        P(None, "tp", None),
        P("tp", None),
        P(None, "tp"),
    )
    return jax.shard_map(
        on_device, mesh=mesh, in_specs=placed, out_specs=P("req", "tp"), check_vma=False
    )
```

```python
import jax
import jax.numpy as jnp
from jax import lax
from jax.experimental import pallas as pl
from jax.experimental.pallas import tpu as pltpu
from jax.sharding import PartitionSpec as P

HD = 88


def layer_norm(inputs, scale_vec, shift_vec):
    widened = inputs.astype(jnp.float32)
    centred = widened - jnp.mean(widened, axis=-1, keepdims=True)
    variance = jnp.mean(centred * centred, axis=-1, keepdims=True)
    return (centred * lax.rsqrt(variance + 1e-06) * scale_vec + shift_vec).astype(jnp.bfloat16)


def grid_positions(seg_row, side_row, first_offset):
    row_len = seg_row.shape[0]
    tok_index = jnp.arange(row_len, dtype=jnp.int32)
    boundary = jnp.concatenate([jnp.ones((1,), dtype=bool), seg_row[1:] != seg_row[:-1]])
    seg_start = lax.cummax(jnp.where(boundary, tok_index, 0), axis=0)
    offset = tok_index - seg_start + jnp.where(seg_row == 0, first_offset, 0)
    half_side = side_row // 2
    window = offset // 4
    corner = offset % 4
    return (2 * (window // half_side) + corner // 2, 2 * (window % half_side) + corner % 2)


def rotate_pairs(channels, angles, axis_pos):
    quarter = channels.shape[axis_pos] // 2
    first_half = lax.slice_in_dim(channels, 0, quarter, axis=axis_pos)
    second_half = lax.slice_in_dim(channels, quarter, 2 * quarter, axis=axis_pos)
    cosine = jnp.cos(angles)
    sine_tab = jnp.sin(angles)
    return jnp.concatenate(
        [
            first_half * cosine - second_half * sine_tab,
            second_half * cosine + first_half * sine_tab,
        ],
        axis=axis_pos,
    )


def apply_rope(channels, row_angles, col_angles, axis_pos):
    half_width = channels.shape[axis_pos] // 2
    row_part = rotate_pairs(
        lax.slice_in_dim(channels, 0, half_width, axis=axis_pos), row_angles, axis_pos
    )
    col_part = rotate_pairs(
        lax.slice_in_dim(channels, half_width, 2 * half_width, axis=axis_pos), col_angles, axis_pos
    )
    return jnp.concatenate([row_part, col_part], axis=axis_pos)


def attend_tile(q_tile, k_ref, v_ref, head, kt, tile, allowed, state):
    largest, total, acc = state
    keys = k_ref[head, :, pl.ds(kt * tile, tile)]
    vals = v_ref[head, :, pl.ds(kt * tile, tile)]
    scores = lax.dot_general(
        keys, q_tile, (((0,), (0,)), ((), ())), preferred_element_type=jnp.float32
    )
    scores = jnp.where(allowed, scores, -1e30)
    larger = jnp.maximum(largest, jnp.max(scores, axis=0, keepdims=True))
    weights = jnp.exp2(scores - larger)
    decay = jnp.exp2(largest - larger)
    total = total * decay + jnp.sum(weights, axis=0, keepdims=True)
    acc = acc * decay + jnp.dot(
        vals, weights.astype(jnp.bfloat16), preferred_element_type=jnp.float32
    )
    return larger, total, acc


def own_kernel(tile, seg_s, q_ref, k_ref, v_ref, segq_ref, segk_ref, acc_ref, stat_ref):
    qt = pl.program_id(0)
    heads = q_ref.shape[0]
    tiles = k_ref.shape[2] // tile
    q_lo, q_hi = (seg_s[qt * tile], seg_s[qt * tile + tile - 1])
    seg_q = segq_ref[...]
    stat_ref[:, 0:1, :] = jnp.full((heads, 1, tile), -1e30, jnp.float32)
    stat_ref[:, 1:8, :] = jnp.zeros((heads, 7, tile), jnp.float32)
    acc_ref[...] = jnp.zeros_like(acc_ref)
    for kt in range(tiles):
        k_lo, k_hi = (seg_s[kt * tile], seg_s[kt * tile + tile - 1])

        @pl.when((k_lo <= q_hi) & (q_lo <= k_hi))
        def _(kt=kt):
            allowed = segk_ref[kt * tile : (kt + 1) * tile, :] == seg_q
            states = [
                attend_tile(
                    q_ref[h], k_ref, v_ref, h, kt, tile, allowed,
                    (stat_ref[h, 0:1, :], stat_ref[h, 1:2, :], acc_ref[h]),
                )
                for h in range(heads)
            ]
            for h, (largest, total, acc) in enumerate(states):
                stat_ref[h, 0:1, :] = largest
                stat_ref[h, 1:2, :] = total
                acc_ref[h] = acc


def near_kernel(
    tile, seg_s, plan_s, q_ref, before_ref, after_ref, segq_ref, acc0_ref, stat0_ref,
    out_ref, stat_ref, acc_ref,
):
    qt = pl.program_id(0)
    heads = q_ref.shape[0]
    length = before_ref.shape[3]
    tiles = length // tile
    q_lo, q_hi, last = (seg_s[qt * tile], seg_s[qt * tile + tile - 1], seg_s[length - 1])
    from_before, from_after = (plan_s[0, 0], plan_s[0, 1])
    seg_q = segq_ref[...]
    stat_ref[...] = stat0_ref[...]
    acc_ref[...] = acc0_ref[...]

    def step(kv_ref, kt, allowed):
        states = [
            attend_tile(
                q_ref[h], kv_ref.at[0], kv_ref.at[1], h, kt, tile, allowed,
                (stat_ref[h, 0:1, :], stat_ref[h, 1:2, :], acc_ref[h]),
            )
            for h in range(heads)
        ]
        for h, (largest, total, acc) in enumerate(states):
            stat_ref[h, 0:1, :] = largest
            stat_ref[h, 1:2, :] = total
            acc_ref[h] = acc

    for kt in range(tiles):

        @pl.when((q_lo == 0) & ((kt + 1) * tile > length - from_before))
        def _(kt=kt):
            rows = lax.broadcasted_iota(jnp.int32, (tile, tile), 0) + kt * tile
            step(before_ref, kt, (rows >= length - from_before) & (seg_q == 0))

        @pl.when((q_hi == last) & (kt * tile < from_after))
        def _(kt=kt):
            rows = lax.broadcasted_iota(jnp.int32, (tile, tile), 0) + kt * tile
            step(after_ref, kt, (rows < from_after) & (seg_q == last))

    for h in range(heads):
        out_ref[h] = (acc_ref[h] / stat_ref[h, 1:2, :]).astype(out_ref.dtype)


def attend_own(queries, keys, values, segment_ids, tile):
    heads, width, length = queries.shape
    whole = pl.BlockSpec((heads, width, length), lambda t, *_: (0, 0, 0))
    tiled = pl.BlockSpec((heads, width, tile), lambda t, *_: (0, 0, t))
    return pl.pallas_call(
        lambda *refs: own_kernel(tile, *refs),
        out_shape=(
            jax.ShapeDtypeStruct((heads, width, length), jnp.float32),
            jax.ShapeDtypeStruct((heads, 8, length), jnp.float32),
        ),
        grid_spec=pltpu.PrefetchScalarGridSpec(
            num_scalar_prefetch=1,
            grid=(length // tile,),
            in_specs=[
                tiled,
                whole,
                whole,
                pl.BlockSpec((1, tile), lambda t, *_: (0, t)),
                pl.BlockSpec((length, 1), lambda t, *_: (0, 0)),
            ],
            out_specs=(tiled, pl.BlockSpec((heads, 8, tile), lambda t, *_: (0, 0, t))),
        ),
        compiler_params=pltpu.CompilerParams(vmem_limit_bytes=32 * 2**20),
        cost_estimate=pl.CostEstimate(
            flops=4 * heads * length * length * width,
            bytes_accessed=4 * heads * length * width * 2,
            transcendentals=heads * length * length,
        ),
        name="own_attention",
    )(segment_ids, queries, keys, values, segment_ids[None, :], segment_ids[:, None])


def attend_near(queries, before, after, segment_ids, split_plan, acc, stat, tile, part):
    _, heads, width, length = before.shape
    whole = pl.BlockSpec((2, heads, width, length), lambda t, *_: (0, 0, 0, 0))
    tiled = pl.BlockSpec((heads, width, tile), lambda t, *_: (part, 0, t))
    return pl.pallas_call(
        lambda *refs: near_kernel(tile, *refs),
        out_shape=jax.ShapeDtypeStruct((heads, width, length), jnp.bfloat16),
        grid_spec=pltpu.PrefetchScalarGridSpec(
            num_scalar_prefetch=2,
            grid=(length // tile,),
            in_specs=[
                tiled,
                whole,
                whole,
                pl.BlockSpec((1, tile), lambda t, *_: (0, t)),
                tiled,
                pl.BlockSpec((heads, 8, tile), lambda t, *_: (part, 0, t)),
            ],
            out_specs=pl.BlockSpec((heads, width, tile), lambda t, *_: (0, 0, t)),
            scratch_shapes=[
                pltpu.VMEM((heads, 8, tile), jnp.float32),
                pltpu.VMEM((heads, width, tile), jnp.float32),
            ],
        ),
        compiler_params=pltpu.CompilerParams(vmem_limit_bytes=32 * 2**20),
        cost_estimate=pl.CostEstimate(
            flops=4 * heads * length * length * width,
            bytes_accessed=6 * heads * length * width * 2,
            transcendentals=heads * length * length,
        ),
        name="near_attention",
    )(
        segment_ids, split_plan, queries, before, after,
        segment_ids[None, :], acc, stat,
    )


def mix_kernel(ho_a_ref, ho_b_ref, wa_ref, wb_ref, patch_ref, wproj_ref, out_ref, mixed_ref):
    length, width = patch_ref.shape
    block = 256

    def mix(i, carry):
        rows = pl.ds(pl.multiple_of(i * block, block), block)
        total = patch_ref[rows, :].astype(jnp.float32)
        for ho_ref, w_ref in ((ho_a_ref, wa_ref), (ho_b_ref, wb_ref)):
            total = total + lax.dot_general(
                ho_ref[:, rows], w_ref[...], (((0,), (0,)), ((), ())),
                preferred_element_type=jnp.float32,
            )
        for g in range(width // 128):
            mixed_ref[g, rows, :] = total[:, g * 128 : (g + 1) * 128]
        return carry

    lax.fori_loop(0, length // block, mix, 0)
    total = jnp.zeros(out_ref.shape, jnp.float32)
    for corner in range(4):
        part = jnp.concatenate(
            [
                mixed_ref[g, pl.ds(corner, length // 4, stride=4), :].astype(jnp.bfloat16)
                for g in range(width // 128)
            ],
            axis=1,
        )
        total += jnp.dot(
            part,
            wproj_ref[corner * width : (corner + 1) * width, :],
            preferred_element_type=jnp.float32,
        )
    out_ref[...] = total.astype(out_ref.dtype)


def mix_and_project(heads_out, w_out, patches, w_proj):
    length, width = patches.shape
    vmem = pl.BlockSpec(memory_space=pltpu.VMEM)
    return pl.pallas_call(
        mix_kernel,
        out_shape=jax.ShapeDtypeStruct((length // 4, w_proj.shape[1]), jnp.bfloat16),
        in_specs=[vmem] * 6,
        out_specs=vmem,
        scratch_shapes=[pltpu.VMEM((width // 128, length, 128), jnp.float32)],
        compiler_params=pltpu.CompilerParams(vmem_limit_bytes=48 * 2**20),
        name="mix_and_project",
    )(*heads_out, *w_out, patches, w_proj)


def on_device(
    patches,
    segment_ids,
    grid_sides,
    split_plan,
    owner_dev,
    dest_row,
    ln_gain,
    ln_bias,
    w_qkv,
    w_out,
    w_proj,
):
    tok_count = patches.shape[0]
    local_heads = w_qkv.shape[1] // HD
    tile = min(256, tok_count)
    split = w_out.shape[0] // 2
    w_out_all = [
        lax.all_gather(part, "tp", axis=0, tiled=True) for part in (w_out[:split], w_out[split:])
    ]
    normed = layer_norm(patches, ln_gain, ln_bias)
    grid_row, grid_col = grid_positions(segment_ids, grid_sides, split_plan[0, 0])
    quarter = HD // 4
    frequency = 10000.0 ** (-jnp.arange(quarter, dtype=jnp.float32) / quarter)
    row_angles = frequency[:, None] * grid_row.astype(jnp.float32)[None, :]
    col_angles = frequency[:, None] * grid_col.astype(jnp.float32)[None, :]
    mixed_kv = jnp.einsum("td,kcd->kct", normed, w_qkv[1:], preferred_element_type=jnp.float32)
    shaped = mixed_kv.reshape(2, local_heads, HD, tok_count)
    keys = apply_rope(shaped[0], row_angles, col_angles, 1).astype(jnp.bfloat16)
    values = shaped[1].astype(jnp.bfloat16)
    count = lax.axis_size("req")
    up = [(i, i + 1) for i in range(count - 1)]
    down = [(j, i) for i, j in up]
    half = local_heads // 2
    near = []
    for first in (0, half):
        part = jnp.stack([keys[first : first + half], values[first : first + half]])
        near.append((lax.ppermute(part, "req", up), lax.ppermute(part, "req", down)))
    mixed_q = jnp.einsum("td,cd->ct", normed, w_qkv[0], preferred_element_type=jnp.float32)
    mixed_q = mixed_q.reshape(local_heads, HD, tok_count)
    scale = HD ** (-0.5) * 1.4426950408889634
    queries = (apply_rope(mixed_q, row_angles, col_angles, 1) * scale).astype(jnp.bfloat16)
    acc, stat = attend_own(queries, keys, values, segment_ids, tile)
    per_owner = owner_dev.shape[0]
    peer_count = lax.axis_size("req")
    owner_slots = 2 * per_owner // peer_count
    matches = (owner_dev[:, None] == jnp.arange(peer_count, dtype=jnp.int32)[None, :]).astype(
        jnp.int32
    )
    arrival = jnp.sum(jnp.cumsum(matches, axis=0) * matches, axis=1) - 1
    send_slot = owner_dev * owner_slots + arrival
    slots = jnp.arange(peer_count * owner_slots, dtype=jnp.int32)
    hit = slots[:, None] == send_slot[None, :]
    send_dest = jnp.sum(jnp.where(hit, dest_row[None, :] + 1, 0), axis=1) - 1
    acc, stat, w_out_all, near = lax.optimization_barrier(
        (acc, stat, w_out_all, near)
    )
    heads_all = []
    for part, (before, after) in enumerate(near):
        heads_out = attend_near(
            queries, before, after, segment_ids, split_plan, acc, stat, tile, part
        )
        heads_all.append(
            lax.all_gather(heads_out.reshape(half * HD, tok_count), "tp", axis=0, tiled=True)
        )
    projected = mix_and_project(heads_all, w_out_all, patches, w_proj)
    got_dest = lax.all_to_all(send_dest, "req", split_axis=0, concat_axis=0, tiled=True)
    place = (jnp.arange(per_owner, dtype=jnp.int32)[:, None] == got_dest[None, :]).astype(
        jnp.bfloat16
    )
    send_rows = jnp.dot(
        hit.astype(jnp.bfloat16), projected, preferred_element_type=jnp.float32
    ).astype(jnp.bfloat16)
    got_rows = lax.all_to_all(send_rows, "req", split_axis=0, concat_axis=0, tiled=True)
    return jnp.dot(place, got_rows, preferred_element_type=jnp.float32).astype(jnp.bfloat16)


def solution(mesh):
    placed = (
        P("req", None),
        P("req"),
        P("req"),
        P("req", None),
        P("req"),
        P("req"),
        P(),
        P(),
        P(None, "tp", None),
        P("tp", None),
        P(None, "tp"),
    )
    return jax.shard_map(
        on_device, mesh=mesh, in_specs=placed, out_specs=P("req", "tp"), check_vma=False
    )
```
